128 devices in a mesh: grp: 16 (over x, z_hi, core), tp: 8 (over z_lo, y).
Axes of the slice: x: 4, y: 4, z: 4 (z_hi: 2, z_lo: 2; z = z_hi * 2 + z_lo), core: 2. Of those that a mesh axis runs over, the one named last changes fastest.
Arguments:
- residual: bfloat16 [4096, 5120], P('grp', 'tp'), may hold values from -5 to 5
- queries: bfloat16 [128, 32, 8192], P('grp', None, 'tp'), may hold values from -125 to 125
- cache_kv: bfloat16 [128, 2, 2048, 1024], P('grp', None, None, 'tp'), may hold values from -5 to 5
- fresh_kv: bfloat16 [128, 2, 32, 1024], P('grp', None, None, 'tp'), may hold values from -5 to 5
- lengths: int32 [128], replicated, may hold values from 1 to 2048, 87381 in all
- destination_place: int32 [128], replicated, may hold values from 0 to 127, each once
- out_weight: bfloat16 [8192, 5120], P('tp'), may hold values from -0.59765625 to 0.59765625
- norm_gain: bfloat16 [5120], replicated, may hold values from 0.5 to 1.5
- gate_up: bfloat16 [5120, 2, 13312], P('grp', None, 'tp'), may hold values from -0.078125 to 0.078125
- block_of: int32 [16], replicated, may hold values from 0 to 15, each once
Outputs:
- evened_activations: bfloat16 [4096, 5120], P('grp', 'tp')
- gated_activations: bfloat16 [4096, 13312], P('grp', 'tp')
The draws below stay inside these ranges and needn't reach their ends.
Inputs may be any that keep to these rules, and one draw needn't show every extreme that they name: `lengths`: the longest sequence uses exactly 2048 stored positions. `destination_place`: every target slot is named by exactly one sequence. `block_of`: every block is held by exactly one index of grp.
All inputs are finite; a program needn't handle non-finite values.
Results may differ from the reference program's by a relative error of at most 0.0081.
Values may be sent and summed in bfloat16 or wider, within the bound.
No kernel may reach another device: no remote copies, remote signals or barrier semaphores. Data moves between devices by JAX's collectives and lax.ppermute only.
A program may use at most 256 MiB of HBM per device.

```python
import math
import jax
import jax.numpy as jnp
import numpy as np
from jax import lax

EMBED_WIDTH = 5120
HQ = 64
KVH = 8
HD = 128
FF = 13312
RECOMPUTE_LEN = 32
LMAX = 2048
STREAMS_ACTIVE = 128
RECOMPUTE_ALL = 4096
BLOCK = 320
N_GRP = 16


def leading_keys(key):
    return jnp.clip(jax.random.normal(jax.random.fold_in(key, 71), (STREAMS_ACTIVE, KVH * HD), jnp.float32), -5.0, 5.0)


def draw_cache_kv(key, part):
    leading = leading_keys(key)
    key = jax.random.fold_in(key, 3)
    stored = jnp.clip(jax.random.normal(key, (STREAMS_ACTIVE, 2, LMAX, KVH * HD), jnp.float32), -5.0, 5.0)
    stored = stored.at[:, 0, 0, :].set(leading)
    return stored.astype(jnp.bfloat16)


def draw_queries(key, part):
    key = jax.random.fold_in(key, 5)
    drawn = jnp.clip(jax.random.normal(key, (STREAMS_ACTIVE, RECOMPUTE_LEN, HQ * HD), jnp.float32), -5.0, 5.0)
    return drawn.astype(jnp.bfloat16)


def levels(rng, dims, shards, low, high):
    gain, own = 1.0, jax.random.fold_in(rng, 6)
    for dim, parts in shards:
        steps = jnp.exp(jax.random.uniform(jax.random.fold_in(own, dim), (parts,), jnp.float32, low / len(shards), high / len(shards)))
        gain = gain * jnp.repeat(steps, dims[dim] // parts).reshape([-1 if axis == dim else 1 for axis in range(len(dims))])
    return gain


def length_profile(amount, total, limit, lean):
    weights = [(1 << 20) // math.isqrt(rank ** lean) + 1 for rank in range(2, amount + 1)]
    surplus, holding = total - limit - (amount - 1), [1] * (amount - 1)
    while surplus > 0:
        free = [i for i in range(amount - 1) if holding[i] < limit]
        pool, remaining = sum([weights[i] for i in free]), surplus
        for i in free:
            more = min(limit - holding[i], max(1, remaining * weights[i] // pool), surplus)
            holding[i] = holding[i] + more
            surplus = surplus - more
    return np.array([limit] + holding)


def ragged_sizes(own_key, amount, total, most, lean):
    if amount == 2:
        one = jax.random.randint(own_key, (), max(1, total - most), min(most, total - 1) + 1)
        return jnp.stack([one, total - one])
    tallies = jnp.asarray(length_profile(amount, total, most, lean), jnp.int32)
    pairs = (amount - 1) // 2
    giver, sink = tallies[1:1 + 2 * pairs:2], tallies[2:2 + 2 * pairs:2]
    room = jnp.minimum(giver - 1, most - sink)
    moved = jax.random.randint(jax.random.fold_in(own_key, 1), (pairs,), 0, 1 << 20) % (room + 1)
    tallies = tallies.at[1:1 + 2 * pairs:2].set(giver - moved).at[2:2 + 2 * pairs:2].set(sink + moved)
    return tallies[jax.random.permutation(jax.random.fold_in(own_key, 2), amount)]


def scatter_about(own_key, shape, deviation, reach, split=(), held_as=jnp.bfloat16):
    array = jax.random.normal(own_key, shape, jnp.float32) * deviation
    if len(split) > 0:
        array = levels(own_key, shape, split, -0.22, 0.18) * array
    return jnp.clip(array, min=-reach, max=reach).astype(held_as)


def setup_inputs(seed: int = 0) -> dict:
    arg_keys = jax.random.split(jax.random.key(seed), 11)
    return {
        "residual": scatter_about(arg_keys[0], (RECOMPUTE_ALL, EMBED_WIDTH), 1.0, 5.0, ((0, 16), (1, 8))),
        "queries": draw_queries(jax.random.fold_in(arg_keys[10], 71), 0),
        "cache_kv": draw_cache_kv(jax.random.fold_in(arg_keys[10], 71), 0),
        "fresh_kv": scatter_about(arg_keys[3], (STREAMS_ACTIVE, 2, RECOMPUTE_LEN, KVH * HD), 1.0, 5.0, ((0, 16), (3, 8))),
        "lengths": ragged_sizes(arg_keys[4], STREAMS_ACTIVE, STREAMS_ACTIVE * LMAX // 3, LMAX, 2).astype(jnp.int32),
        "destination_place": jax.random.permutation(arg_keys[5], STREAMS_ACTIVE).astype(jnp.int32),
        "out_weight": scatter_about(arg_keys[6], (HQ * HD, EMBED_WIDTH), 0.1, 0.59765625, ((0, 8),)),
        "norm_gain": jnp.clip(1.0 + 0.1 * jax.random.normal(arg_keys[7], (EMBED_WIDTH,), jnp.float32), 0.5, 1.5).astype(jnp.bfloat16),
        "gate_up": scatter_about(arg_keys[8], (EMBED_WIDTH, 2, FF), EMBED_WIDTH ** -0.5, 0.078125, ((0, 16), (2, 8))),
        "block_of": jax.random.permutation(arg_keys[9], N_GRP).astype(jnp.int32),
    }


def attend_sequence(packed):
    queries, stored, fresh_rows, seq_length = packed
    key_rows = jnp.concatenate([stored[0], fresh_rows[0]], axis=0).astype(jnp.float32).reshape(LMAX + RECOMPUTE_LEN, KVH, HD)
    values = jnp.concatenate([stored[1], fresh_rows[1]], axis=0).astype(jnp.float32).reshape(LMAX + RECOMPUTE_LEN, KVH, HD)
    grouped = queries.astype(jnp.float32).reshape(RECOMPUTE_LEN, KVH, HQ // KVH, HD)
    scores = jnp.einsum('rkgd,nkd->kgrn', grouped, key_rows) * HD ** (-0.5)
    position = jnp.arange(LMAX + RECOMPUTE_LEN, dtype=jnp.int32)
    row_index = jnp.arange(RECOMPUTE_LEN, dtype=jnp.int32)
    visible = jnp.where(position[None, :] < LMAX, position[None, :] < seq_length, position[None, :] - LMAX <= row_index[:, None])
    scores = jnp.where(visible, scores, -jnp.inf)
    probability = jax.nn.softmax(scores, axis=-1).astype(jnp.bfloat16)
    context = jnp.einsum('kgrn,nkd->rkgd', probability.astype(jnp.float32), values)
    return context.reshape(RECOMPUTE_LEN, HQ * HD).astype(jnp.bfloat16)

def reference(residual, queries, cache_kv, fresh_kv, lengths, destination_place, out_weight, norm_gain, gate_up, block_of):
    context = lax.map(attend_sequence, (queries, cache_kv, fresh_kv, lengths))
    context = context.reshape(RECOMPUTE_ALL, HQ * HD)
    attended = jnp.dot(context, out_weight, preferred_element_type=jnp.float32)
    combined_partials = (residual.astype(jnp.float32) + attended).astype(jnp.bfloat16).reshape(STREAMS_ACTIVE, RECOMPUTE_LEN, EMBED_WIDTH)
    evened_activations = jnp.zeros((STREAMS_ACTIVE, RECOMPUTE_LEN, EMBED_WIDTH), jnp.bfloat16).at[destination_place].set(combined_partials).reshape(RECOMPUTE_ALL, EMBED_WIDTH)
    widened_entries = evened_activations.astype(jnp.float32)
    mean_square = lax.optimization_barrier(jnp.mean(widened_entries * widened_entries, axis=-1, keepdims=True))
    normed = (widened_entries * lax.rsqrt(mean_square + 1e-06) * norm_gain.astype(jnp.float32)[None, :]).astype(jnp.bfloat16)
    ordered = jnp.take(normed.reshape(RECOMPUTE_ALL, N_GRP, BLOCK), block_of, axis=1).reshape(RECOMPUTE_ALL, EMBED_WIDTH)
    projected = jnp.dot(ordered, gate_up.reshape(EMBED_WIDTH, 2 * FF), preferred_element_type=jnp.float32).reshape(RECOMPUTE_ALL, 2, FF)
    gated_activations = (jax.nn.silu(projected[:, 0, :]) * projected[:, 1, :]).astype(jnp.bfloat16)
    return (evened_activations, gated_activations)
```

```python
import functools

import jax
import jax.numpy as jnp
from jax import lax
from jax.experimental import pallas as pl
from jax.experimental.pallas import tpu as pltpu
from jax.sharding import Mesh, PartitionSpec as P

AX = ("x", "zh", "c", "zl", "y")
SIZES = dict(x=4, zh=2, c=2, zl=2, y=4)
BF = jnp.bfloat16
F32 = jnp.float32
HD = 128
HEADS = 8
SEQS = 8
ROWS = 32
LMAX = 2048
KB = 512
NB = LMAX // KB
D = 5120
DT = 640
BLK = 320
FT = 1664
NEG = -1e30
EPS = 1e-6
VM = pl.BlockSpec(memory_space=pltpu.VMEM)
SM = pl.BlockSpec(memory_space=pltpu.SMEM)
ANY = pl.BlockSpec(memory_space=pl.ANY)


def permute(value, axes, move):
    sizes = [SIZES[a] for a in axes]
    total = 1
    for n in sizes:
        total *= n
    pairs = []
    for i in range(total):
        coords, rest = [], i
        for n in reversed(sizes):
            coords.append(rest % n)
            rest //= n
        target = move(*reversed(coords))
        j = 0
        for n, q in zip(sizes, target):
            j = j * n + q
        pairs.append((i, j))
    return lax.ppermute(value, axes, pairs)


def along_x(value, k):
    return permute(value, ("x",), lambda x: ((x + k) % 4,))


def along_y(value, k):
    return permute(value, ("y",), lambda y: ((y + k) % 4,))


def along_z(value, k):
    def move(zh, zl):
        z = (zh * 2 + zl + k) % 4
        return (z // 2, z % 2)

    return permute(value, ("zh", "zl"), move)


def swap(value, axis):
    return permute(value, (axis,), lambda q: (1 - q,))


def shuffle(row, inner):
    return (row // 4 % 8) * 32 + (row // 32) * 4 + row % 4


def one_hot(n):
    out = lax.broadcasted_iota(jnp.int32, (n, n), 0)
    src = lax.broadcasted_iota(jnp.int32, (n, n), 1)
    return (shuffle(out, None) == src).astype(BF)


def front_kernel(len_ref, q_ref, fresh_ref, cache_ref, ow_ref, out_ref, kv, ow, ctx, kv_sem, ow_sem):
    def kv_copy(s, b):
        part = pl.ds(b * KB, KB)
        return pltpu.make_async_copy(
            cache_ref.at[s, :, part, :], kv.at[s, :, part, :], kv_sem.at[s, b]
        )

    for s in range(SEQS):
        for b in range(NB):

            @pl.when(b * KB < len_ref[s])
            def _(s=s, b=b):
                kv_copy(s, b).start()

    ow_copy = pltpu.make_async_copy(ow_ref, ow, ow_sem)
    ow_copy.start()
    factor = HD ** -0.5 * 1.4426950408889634
    nt = (((1,), (1,)), ((), ()))
    nn = (((1,), (0,)), ((), ()))

    def sequence(s, _):
        length = len_ref[s]
        rows = q_ref[s]
        q = jnp.concatenate([rows[:, h * HD : (h + 1) * HD] for h in range(HEADS)], axis=0)
        scores = lax.dot_general(q, fresh_ref[s, 0], nt, preferred_element_type=F32) * factor
        i = lax.broadcasted_iota(jnp.int32, scores.shape, 0) % ROWS
        j = lax.broadcasted_iota(jnp.int32, scores.shape, 1)
        scores = jnp.where(j <= i, scores, NEG)
        high = jnp.max(scores, axis=1, keepdims=True)
        p = jnp.exp2(scores - high)
        total = jnp.sum(p, axis=1, keepdims=True)
        acc = lax.dot_general(p.astype(BF), fresh_ref[s, 1], nn, preferred_element_type=F32)

        def block(b, carry):
            high, total, acc = carry
            kv_copy(s, b).wait()
            start = pl.multiple_of(b * KB, KB)
            k = kv[s, 0, pl.ds(start, KB), :]
            v = kv[s, 1, pl.ds(start, KB), :]
            scores = lax.dot_general(q, k, nt, preferred_element_type=F32) * factor
            pos = lax.broadcasted_iota(jnp.int32, scores.shape, 1)
            scores = jnp.where(pos < length - start, scores, NEG)
            new = jnp.maximum(high, jnp.max(scores, axis=1, keepdims=True))
            old = jnp.exp2(high - new)
            p = jnp.exp2(scores - new)
            total = total * old + jnp.sum(p, axis=1, keepdims=True)
            acc = acc * old + lax.dot_general(p.astype(BF), v, nn, preferred_element_type=F32)
            return new, total, acc

        high, total, acc = lax.fori_loop(0, (length + KB - 1) // KB, block, (high, total, acc))
        done = (acc / total).astype(BF)
        at = pl.ds(pl.multiple_of(s * ROWS, ROWS), ROWS)
        for h in range(HEADS):
            ctx[at, h * HD : (h + 1) * HD] = done[h * ROWS : (h + 1) * ROWS, :]
        return 0

    lax.fori_loop(0, SEQS, sequence, 0)
    mixed = jnp.dot(one_hot(256), ctx[...], preferred_element_type=F32).astype(BF)
    ow_copy.wait()
    for t in range(8):
        out_ref[t] = jnp.dot(
            mixed, ow[:, t * DT : (t + 1) * DT], preferred_element_type=F32
        ).astype(BF)


def front(lengths, queries, fresh, cache, out_weight):
    return pl.pallas_call(
        front_kernel,
        out_shape=jax.ShapeDtypeStruct((8, 256, DT), BF),
        in_specs=[SM, VM, VM, ANY, ANY],
        out_specs=VM,
        scratch_shapes=[
            pltpu.VMEM((SEQS, 2, LMAX, HD), BF),
            pltpu.VMEM((1024, D), BF),
            pltpu.VMEM((256, 1024), BF),
            pltpu.SemaphoreType.DMA((SEQS, NB)),
            pltpu.SemaphoreType.DMA,
        ],
        compiler_params=pltpu.CompilerParams(vmem_limit_bytes=48 * 2**20),
        name="attend_project",
    )(lengths, queries, fresh, cache, out_weight)


def feed_kernel(pos_ref, block_ref, src_ref, gain_ref, *refs):
    first, second, weights = refs[0:4], refs[4:8], refs[8:12]
    out_ref, act, normed, w, act_sem, w_sem = refs[12:]
    x, zh, c, zl, y = (pos_ref[i] for i in range(5))
    z = zh * 2 + zl
    copies = []
    for dz in range(2):
        for dc in range(2):
            for j, dx in enumerate((0, 3, 1, 2)):
                g = (x + dx) % 4 * 4 + (zh + dz) % 2 * 2 + (c + dc) % 2
                at = pl.multiple_of(block_ref[g] * BLK, BLK)
                copies.append(
                    pltpu.make_async_copy(
                        weights[dz * 2 + dc].at[pl.ds(j * BLK, BLK), :],
                        w.at[pl.ds(at, BLK), :],
                        w_sem.at[dz * 8 + dc * 4 + j],
                    )
                )
    pieces = []
    for half, group in enumerate((first, second)):
        for a, da in enumerate((0, 3, 1, 2)):
            for b, db in enumerate((0, 3, 1, 2)):
                dz, dy = (da, db) if half == 0 else (db, da)
                zz = (z + dz) % 4
                t = zz % 2 * 4 + (y + dy) % 4
                row = pl.multiple_of(zz // 2 * 256 + half * 128, 128)
                col = pl.multiple_of(t * DT, 128)
                pieces.append(
                    pltpu.make_async_copy(
                        group[a].at[b],
                        act.at[pl.ds(row, 128), pl.ds(col, DT)],
                        act_sem.at[half * 16 + a * 4 + b],
                    )
                )
    for copy in pieces + copies:
        copy.start()
    for copy in pieces:
        copy.wait()
    gain = gain_ref[...].astype(F32)
    for r in range(0, 512, 64):
        rows = act[r : r + 64, :].astype(F32)
        inverse = lax.rsqrt(jnp.sum(rows * rows, axis=1, keepdims=True) / D + EPS)
        normed[r : r + 64, :] = (rows * inverse * gain).astype(BF)
    for copy in copies:
        copy.wait()
    own = pl.multiple_of((zl * 4 + y) * DT, 128)
    flag = zh == 0
    for r in range(0, 512, 256):
        proj = jnp.dot(normed[r : r + 256, :], w[...], preferred_element_type=F32)
        g, u, m = proj[:, :768], proj[:, 768:1536], proj[:, 1536:]
        out_ref[r : r + 256, 0:768] = (g / (1 + jnp.exp(-g)) * u).astype(BF)
        tail = (m / (1 + jnp.exp(-m)) * pltpu.roll(m, 64, 1)).astype(BF).astype(F32)
        low = act[r : r + 256, pl.ds(own, 256)]
        mid = act[r : r + 256, pl.ds(pl.multiple_of(own + 256, 128), 128)].astype(F32)
        high = act[r : r + 256, pl.ds(pl.multiple_of(own + 384, 128), 256)]
        lane = lax.broadcasted_iota(jnp.int32, mid.shape, 1)
        mid = jnp.where(flag, pltpu.roll(mid, 64, 1), mid)
        out_ref[r : r + 256, 768:896] = jnp.where(lane < 64, tail, mid).astype(BF)
        out_ref[r : r + 256, 896:1152] = jnp.where(flag, low.astype(F32), high.astype(F32)).astype(BF)
    hot = (src_ref[...] == lax.broadcasted_iota(jnp.int32, (512, 512), 1)).astype(BF)
    out_ref[...] = jnp.dot(hot, out_ref[...], preferred_element_type=F32).astype(BF)


def feed(pos, block_of, src, gain, first, second, weights):
    return pl.pallas_call(
        feed_kernel,
        out_shape=jax.ShapeDtypeStruct((512, 1152), BF),
        in_specs=[SM, SM, VM, VM] + [ANY] * 12,
        out_specs=VM,
        scratch_shapes=[
            pltpu.VMEM((512, D), BF),
            pltpu.VMEM((512, D), BF),
            pltpu.VMEM((D, FT), BF),
            pltpu.SemaphoreType.DMA((32,)),
            pltpu.SemaphoreType.DMA((16,)),
        ],
        compiler_params=pltpu.CompilerParams(vmem_limit_bytes=56 * 2**20),
        name="feed_forward",
    )(pos, block_of, src, gain, *first, *second, *weights)


def finish_kernel(in_ref, even_ref, gated_ref):
    hot = one_hot(256)
    halves = []
    for zh in range(2):
        rows = jnp.concatenate([in_ref[x * 4 + zh * 2 + c] for x in range(4) for c in range(2)], axis=0)
        halves.append(jnp.dot(hot, rows, preferred_element_type=F32))
    a, b = halves
    lane = lax.broadcasted_iota(jnp.int32, (256, 128), 1)
    gated_ref[:, 0:768] = a[:, 0:768].astype(BF)
    gated_ref[:, 896:1664] = b[:, 0:768].astype(BF)
    am, bm = a[:, 768:896], b[:, 768:896]
    gated_ref[:, 768:896] = jnp.where(lane < 64, am, pltpu.roll(bm, 64, 1)).astype(BF)
    even_ref[:, 0:256] = a[:, 896:1152].astype(BF)
    even_ref[:, 256:384] = jnp.where(lane < 64, pltpu.roll(am, 64, 1), bm).astype(BF)
    even_ref[:, 384:640] = b[:, 896:1152].astype(BF)


def finish(parts):
    return pl.pallas_call(
        finish_kernel,
        out_shape=(jax.ShapeDtypeStruct((256, DT), BF), jax.ShapeDtypeStruct((256, FT), BF)),
        in_specs=[VM],
        out_specs=(VM, VM),
        compiler_params=pltpu.CompilerParams(vmem_limit_bytes=32 * 2**20),
        name="finish",
    )(parts)


def portion(gate_up, h):
    wide = [lax.dynamic_slice_in_dim(gate_up[:, j, :], h * 896, 768, 1) for j in range(2)]
    thin = [lax.dynamic_slice_in_dim(gate_up[:, j, :], 768 + h * 64, 64, 1) for j in range(2)]
    return jnp.concatenate(wide + thin, axis=1)


def per_device(
    residual, queries, cache_kv, fresh_kv, lengths, destination_place, out_weight, norm_gain, gate_up, block_of
):
    x, zh, c, zl, y = (lax.axis_index(a) for a in AX)
    pos = jnp.stack([x, zh, c, zl, y]).astype(jnp.int32)
    group = x * 4 + zh * 2 + c

    own = portion(gate_up, zh)
    other = portion(gate_up, 1 - zh)
    w0 = own
    w0p, w0m = along_x(w0, 1), along_x(w0, -1)
    w1 = swap(other, "zh")

    own_lengths = lax.dynamic_slice_in_dim(lengths, group * SEQS, SEQS, 0)
    terms = front(own_lengths, queries, fresh_kv, cache_kv, out_weight)

    terms, w0p, w0m, w1 = lax.optimization_barrier((terms, w0p, w0m, w1))
    w1p, w1m = along_x(w1, 1), along_x(w1, -1)
    w0a, w0b = along_x(w0p[:160], 1), along_x(w0m[160:], -1)

    terms = lax.all_to_all(terms, ("zl", "y"), 0, 0, tiled=True)
    mixed_residual = residual.reshape(8, 8, 4, DT).transpose(1, 0, 2, 3).reshape(256, DT)
    even = (mixed_residual.astype(F32) + jnp.sum(terms.astype(F32), axis=0)).astype(BF)

    even, w1p, w1m, w0a, w0b = lax.optimization_barrier((even, w1p, w1m, w0a, w0b))
    w1a, w1b = along_x(w1p[:160], 1), along_x(w1m[160:], -1)
    w0 = jnp.concatenate([w0, w0p, w0m, w0a, w0b], axis=0)
    w0s = swap(w0, "c")

    even = lax.all_to_all(even, ("x", "c"), 0, 0, tiled=True)

    h1, h2 = even[:128], even[128:]
    g1 = jnp.stack([h1, along_y(h1, 1), along_y(h1, -1), along_y(h1, 2)])
    g2 = jnp.stack([h2, along_z(h2, 1), along_z(h2, -1), along_z(h2, 2)])
    g1, g2, w1a, w1b = lax.optimization_barrier((g1, g2, w1a, w1b))
    w1 = jnp.concatenate([w1, w1p, w1m, w1a, w1b], axis=0)
    w1s = swap(w1, "c")
    first = [g1, along_z(g1, 1), along_z(g1, -1), along_z(g1, 2)]
    second = [g2, along_y(g2, 1), along_y(g2, -1), along_y(g2, 2)]

    slots = lax.iota(jnp.int32, 128)
    seq = jnp.sum(
        jnp.where(destination_place[None, :] == slots[:, None], slots[None, :], 0), axis=1
    )
    g = seq // 8
    base = (g // 2 % 2) * 256 + (g // 4 * 2 + g % 2) * 32 + seq % 8 * 4
    src = (base[:, None] + lax.iota(jnp.int32, 4)[None, :]).reshape(512, 1)
    both = feed(pos, block_of, src, norm_gain.reshape(1, D), first, second, [w0, w0s, w1, w1s])
    both = lax.all_to_all(both.reshape(16, 32, 1152), ("x", "zh", "c"), 0, 0, tiled=True)
    return finish(both)


def solution(mesh):
    inner = Mesh(mesh.devices.reshape(tuple(SIZES[a] for a in AX)), AX)
    grp, tp = ("x", "zh", "c"), ("zl", "y")
    return jax.shard_map(
        per_device,
        mesh=inner,
        in_specs=(
            P(grp, tp),
            P(grp, None, tp),
            P(grp, None, None, tp),
            P(grp, None, None, tp),
            P(),
            P(),
            P(tp, None),
            P(),
            P(grp, None, tp),
            P(),
        ),
        out_specs=(P(grp, tp), P(grp, tp)),
        check_vma=False,
    )
```

```python
import functools

import jax
import jax.numpy as jnp
from jax import lax
from jax.experimental import pallas as pl
from jax.experimental.pallas import tpu as pltpu
from jax.sharding import Mesh, PartitionSpec as P

AX = ("x", "zh", "c", "zl", "y")
SIZES = dict(x=4, zh=2, c=2, zl=2, y=4)
BF = jnp.bfloat16
F32 = jnp.float32
HD = 128
HEADS = 8
SEQS = 8
ROWS = 32
LMAX = 2048
KB = 512
NB = LMAX // KB
D = 5120
DT = 640
BLK = 320
FT = 1664
NEG = -1e30
EPS = 1e-6
NC = 1
RR = 4 // NC
CR = 64 * RR
NH = 896
VM = pl.BlockSpec(memory_space=pltpu.VMEM)
SM = pl.BlockSpec(memory_space=pltpu.SMEM)
ANY = pl.BlockSpec(memory_space=pl.ANY)


def permute(value, axes, move):
    sizes = [SIZES[a] for a in axes]
    total = 1
    for n in sizes:
        total *= n
    pairs = []
    for i in range(total):
        coords, rest = [], i
        for n in reversed(sizes):
            coords.append(rest % n)
            rest //= n
        target = move(*reversed(coords))
        j = 0
        for n, q in zip(sizes, target):
            j = j * n + q
        pairs.append((i, j))
    return lax.ppermute(value, axes, pairs)


def along_x(value, k):
    return permute(value, ("x",), lambda x: ((x + k) % 4,))


def along_y(value, k):
    return permute(value, ("y",), lambda y: ((y + k) % 4,))


def along_z(value, k):
    def move(zh, zl):
        z = (zh * 2 + zl + k) % 4
        return (z // 2, z % 2)

    return permute(value, ("zh", "zl"), move)


def swap(value, axis):
    return permute(value, (axis,), lambda q: (1 - q,))


def one_hot(n, source):
    out = lax.broadcasted_iota(jnp.int32, (n, n), 0)
    src = lax.broadcasted_iota(jnp.int32, (n, n), 1)
    return (source(out) == src).astype(BF)


def spread(row):
    return row // RR % 8 * ROWS + row // (8 * RR) % 8 * 4 + row // CR * RR + row % RR


def gather(row):
    return row // RR % NC * CR + row // 4 % 8 * (8 * RR) + row // ROWS * RR + row % RR


def front_kernel(len_ref, q_ref, fresh_ref, res_ref, cache_ref, ow_ref, *refs):
    out_refs, (kv, ow, ctx, kv_sem, ow_sem) = refs[:NC], refs[NC:]
    def kv_copy(s, b):
        part = pl.ds(b * KB, KB)
        return pltpu.make_async_copy(
            cache_ref.at[s, :, part, :], kv.at[s, :, part, :], kv_sem.at[s, b]
        )

    for s in range(SEQS):
        for b in range(NB):

            @pl.when(b * KB < len_ref[s])
            def _(s=s, b=b):
                kv_copy(s, b).start()

    ow_copy = pltpu.make_async_copy(ow_ref, ow, ow_sem)
    ow_copy.start()
    factor = HD ** -0.5 * 1.4426950408889634
    nt = (((1,), (1,)), ((), ()))
    nn = (((1,), (0,)), ((), ()))

    def sequence(s, _):
        length = len_ref[s]
        rows = q_ref[s]
        q = jnp.concatenate([rows[:, h * HD : (h + 1) * HD] for h in range(HEADS)], axis=0)
        scores = lax.dot_general(q, fresh_ref[s, 0], nt, preferred_element_type=F32) * factor
        i = lax.broadcasted_iota(jnp.int32, scores.shape, 0) % ROWS
        j = lax.broadcasted_iota(jnp.int32, scores.shape, 1)
        scores = jnp.where(j <= i, scores, NEG)
        high = jnp.max(scores, axis=1, keepdims=True)
        p = jnp.exp2(scores - high)
        total = jnp.sum(p, axis=1, keepdims=True)
        acc = lax.dot_general(p.astype(BF), fresh_ref[s, 1], nn, preferred_element_type=F32)

        def block(b, carry):
            high, total, acc = carry
            kv_copy(s, b).wait()
            start = pl.multiple_of(b * KB, KB)
            k = kv[s, 0, pl.ds(start, KB), :]
            v = kv[s, 1, pl.ds(start, KB), :]
            scores = lax.dot_general(q, k, nt, preferred_element_type=F32) * factor
            pos = lax.broadcasted_iota(jnp.int32, scores.shape, 1)
            scores = jnp.where(pos < length - start, scores, NEG)
            new = jnp.maximum(high, jnp.max(scores, axis=1, keepdims=True))
            old = jnp.exp2(high - new)
            p = jnp.exp2(scores - new)
            total = total * old + jnp.sum(p, axis=1, keepdims=True)
            acc = acc * old + lax.dot_general(p.astype(BF), v, nn, preferred_element_type=F32)
            return new, total, acc

        high, total, acc = lax.fori_loop(0, (length + KB - 1) // KB, block, (high, total, acc))
        done = (acc / total).astype(BF)
        at = pl.ds(pl.multiple_of(s * ROWS, ROWS), ROWS)
        for h in range(HEADS):
            ctx[at, h * HD : (h + 1) * HD] = done[h * ROWS : (h + 1) * ROWS, :]
        return 0

    lax.fori_loop(0, SEQS, sequence, 0)
    hot = one_hot(256, spread)
    mixed = jnp.dot(hot, ctx[...], preferred_element_type=F32).astype(BF)
    residual = jnp.dot(hot, res_ref[...], preferred_element_type=F32)
    ow_copy.wait()
    for t in range(8):
        terms = jnp.dot(mixed, ow[:, t * DT : (t + 1) * DT], preferred_element_type=F32)
        terms = (terms + jnp.where(len_ref[SEQS] == t, residual, 0.0)).astype(BF)
        for q in range(NC):
            out_refs[q][t] = terms[q * CR : (q + 1) * CR]


def front(lengths, queries, fresh, residual, cache, out_weight):
    return pl.pallas_call(
        front_kernel,
        out_shape=[jax.ShapeDtypeStruct((8, CR, DT), BF)] * NC,
        in_specs=[SM, VM, VM, VM, ANY, ANY],
        out_specs=[VM] * NC,
        scratch_shapes=[
            pltpu.VMEM((SEQS, 2, LMAX, HD), BF),
            pltpu.VMEM((1024, D), BF),
            pltpu.VMEM((256, 1024), BF),
            pltpu.SemaphoreType.DMA((SEQS, NB)),
            pltpu.SemaphoreType.DMA,
        ],
        compiler_params=pltpu.CompilerParams(vmem_limit_bytes=48 * 2**20),
        name="attend_project",
    )(lengths, queries, fresh, residual, cache, out_weight)


def feed_kernel(pos_ref, block_ref, src_ref, gain_ref, *refs):
    arrived, (near_ref, far_ref, out_ref, act, normed, w, act_sem, w_sem) = refs[:10], refs[10:]
    zh, tp, z, y = (pos_ref[i] for i in range(4))
    half = CR // 2
    steps = (0, 3, 1, 2)
    pieces = []
    for h in range(2):
        own, one, two, low, high = arrived[h * 5 : h * 5 + 5]
        blocks = [(own, j, 0, j) for j in range(4)]
        blocks += [(one, j, 3, j) for j in range(4)] + [(two, j, 1, j) for j in range(4)]
        blocks += [(low, j, 2, j) for j in range(2)] + [(high, j, 2, j + 2) for j in range(2)]
        for n, (ref, at, outer, j) in enumerate(blocks):
            dz, dy = (outer, steps[j]) if h == 0 else (steps[j], outer)
            zz = (z + dz) % 4
            row = pl.multiple_of(zz // 2 * CR + h * half, half)
            col = pl.multiple_of((zz % 2 * 4 + (y + dy) % 4) * DT, 128)
            pieces.append(
                pltpu.make_async_copy(
                    ref.at[at], act.at[pl.ds(row, half), pl.ds(col, DT)], act_sem.at[h * 16 + n]
                )
            )
    for copy in pieces:
        copy.start()

    tiles = ((0, 256), (256, 256), (512, 256), (768, 128))

    def weights(n):
        at, size = tiles[n]
        copies = []
        for dz, source in enumerate((near_ref, far_ref)):
            for i in range(8):
                g = i // 2 * 4 + (zh + dz) % 2 * 2 + i % 2
                row = pl.multiple_of(block_ref[g] * BLK, BLK)
                copies.append(
                    pltpu.make_async_copy(
                        source.at[i, :, :, pl.ds(at, size)],
                        w.at[:, pl.ds(row, BLK), pl.ds(at, size)],
                        w_sem.at[n, dz * 8 + i],
                    )
                )
        return copies

    for copy in weights(0):
        copy.start()
    for copy in pieces:
        copy.wait()
    for copy in weights(1):
        copy.start()
    gain = gain_ref[...].astype(F32)
    for r in range(0, 2 * CR, 64):
        rows = act[r : r + 64, :].astype(F32)
        inverse = lax.rsqrt(jnp.sum(rows * rows, axis=1, keepdims=True) / D + EPS)
        normed[r : r + 64, :] = (rows * inverse * gain).astype(BF)
    lhs = normed[...]
    for n, (at, size) in enumerate(tiles):
        for copy in weights(n):
            copy.wait()
        if n + 2 < len(tiles):
            for copy in weights(n + 2):
                copy.start()
        g = jnp.dot(lhs, w[0, :, at : at + size], preferred_element_type=F32)
        u = jnp.dot(lhs, w[1, :, at : at + size], preferred_element_type=F32)
        out_ref[:, at : at + size] = (g / (1 + jnp.exp(-g)) * u).astype(BF)
    own = pl.multiple_of(tp * DT, 128)
    flag = zh == 0
    mid = act[:, pl.ds(pl.multiple_of(own + 256, 128), 128)]
    low = act[:, pl.ds(own, 256)]
    high = act[:, pl.ds(pl.multiple_of(own + 384, 128), 256)]
    out_ref[:, 896:1152] = jnp.where(flag, low.astype(F32), high.astype(F32)).astype(BF)

    @pl.when(jnp.logical_not(flag))
    def _():
        out_ref[:, 0:128] = mid

    hot = (src_ref[...] == lax.broadcasted_iota(jnp.int32, (2 * CR, 2 * CR), 1)).astype(BF)
    out_ref[...] = jnp.dot(hot, out_ref[...], preferred_element_type=F32).astype(BF)


def feed(pos, block_of, src, gain, arrived, near, far):
    return pl.pallas_call(
        feed_kernel,
        out_shape=jax.ShapeDtypeStruct((2 * CR, 1152), BF),
        in_specs=[SM, SM, VM, VM] + [ANY] * 12,
        out_specs=VM,
        scratch_shapes=[
            pltpu.VMEM((2 * CR, D), BF),
            pltpu.VMEM((2 * CR, D), BF),
            pltpu.VMEM((2, D, NH), BF),
            pltpu.SemaphoreType.DMA((32,)),
            pltpu.SemaphoreType.DMA((4, 16)),
        ],
        compiler_params=pltpu.CompilerParams(vmem_limit_bytes=56 * 2**20),
        name="feed_forward",
    )(pos, block_of, src, gain, *arrived, near, far)


def finish_kernel(*refs):
    in_refs, (even_ref, gated_ref) = refs[:NC], refs[NC:]
    hot = one_hot(256, gather)
    halves = []
    for zh in range(2):
        rows = jnp.concatenate(
            [r[x * 4 + zh * 2 + c] for r in in_refs for x in range(4) for c in range(2)], axis=0
        )
        halves.append(jnp.dot(hot, rows, preferred_element_type=F32).astype(BF))
    a, b = halves
    gated_ref[:, 0:896] = a[:, 0:896]
    gated_ref[:, 896:1664] = b[:, 128:896]
    even_ref[:, 0:256] = a[:, 896:1152]
    even_ref[:, 256:384] = b[:, 0:128]
    even_ref[:, 384:640] = b[:, 896:1152]


def finish(parts):
    return pl.pallas_call(
        finish_kernel,
        out_shape=(jax.ShapeDtypeStruct((256, DT), BF), jax.ShapeDtypeStruct((256, FT), BF)),
        in_specs=[VM] * NC,
        out_specs=(VM, VM),
        compiler_params=pltpu.CompilerParams(vmem_limit_bytes=32 * 2**20),
        name="finish",
    )(*parts)


def per_device(
    residual, queries, cache_kv, fresh_kv, lengths, destination_place, out_weight, norm_gain, gate_up, block_of
):
    x, zh, c, zl, y = (lax.axis_index(a) for a in AX)
    pos = jnp.stack([zh, zl * 4 + y, zh * 2 + zl, y]).astype(jnp.int32)
    group = x * 4 + zh * 2 + c

    both = lax.optimization_barrier(gate_up.transpose(1, 0, 2))
    left, right = both[:, :, :NH], both[:, :, FT - NH :]
    own = jnp.where(zh == 0, left, right)
    other = jnp.where(zh == 0, right, left)
    near = lax.all_gather(own, ("x", "c"), axis=0)
    lower, upper = swap(other[:, : BLK // 2], "zh"), swap(other[:, BLK // 2 :], "zh")

    own_lengths = lax.dynamic_slice_in_dim(lengths, group * SEQS, SEQS, 0)
    scalars = jnp.concatenate([own_lengths, pos[1:2]])
    terms = front(scalars, queries, fresh_kv, residual, cache_kv, out_weight)
    lower, *terms = lax.optimization_barrier((lower, *terms))

    slots = lax.iota(jnp.int32, 128)
    seq = jnp.sum(
        jnp.where(destination_place[None, :] == slots[:, None], slots[None, :], 0), axis=1
    )
    g = seq // 8
    base = (g // 2 % 2) * CR + (g // 4 * 2 + g % 2) * (8 * RR) + seq % 8 * RR
    src = (base[:, None] + lax.iota(jnp.int32, RR)[None, :]).reshape(2 * CR, 1)
    gain = norm_gain.reshape(1, D)

    parts = []
    for q in range(NC):
        got = lax.all_to_all(terms[q], ("zl", "y"), 0, 0, tiled=True)
        even = jnp.sum(got.astype(F32), axis=0).astype(BF)
        even = lax.all_to_all(even, ("x", "c"), 0, 0, tiled=True)
        if q == 0:
            upper, even = lax.optimization_barrier((upper, even))
            other = jnp.concatenate([lower, upper], axis=1)
            far = lax.all_gather(other, ("x", "c"), axis=0)
        h1, h2 = even[: CR // 2], even[CR // 2 :]
        g1 = jnp.stack([h1, along_y(h1, 1), along_y(h1, -1), along_y(h1, 2)])
        g2 = jnp.stack([h2, along_z(h2, 1), along_z(h2, -1), along_z(h2, 2)])
        g1, g2 = lax.optimization_barrier((g1, g2))
        a1, a2, b1, b2 = along_z(g1, 1), along_z(g1, -1), along_y(g2, 1), along_y(g2, -1)
        a1, a2, b1, b2 = lax.optimization_barrier((a1, a2, b1, b2))
        arrived = [g1, a1, a2, along_z(a1[:2], 1), along_z(a2[2:], -1)]
        arrived += [g2, b1, b2, along_y(b1[:2], 1), along_y(b2[2:], -1)]
        mixed = feed(pos, block_of, src, gain, arrived, near, far)
        parts.append(lax.all_to_all(mixed.reshape(16, 8 * RR, 1152), ("x", "zh", "c"), 0, 0, tiled=True))
    return finish(parts)


def solution(mesh):
    inner = Mesh(mesh.devices.reshape(tuple(SIZES[a] for a in AX)), AX)
    grp, tp = ("x", "zh", "c"), ("zl", "y")
    return jax.shard_map(
        per_device,
        mesh=inner,
        in_specs=(
            P(grp, tp),
            P(grp, None, tp),
            P(grp, None, None, tp),
            P(grp, None, None, tp),
            P(),
            P(),
            P(tp, None),
            P(),
            P(grp, None, tp),
            P(),
        ),
        out_specs=(P(grp, tp), P(grp, tp)),
        check_vma=False,
    )
```

```python
import functools

import jax
import jax.numpy as jnp
from jax import lax
from jax.experimental import pallas as pl
from jax.experimental.pallas import tpu as pltpu
from jax.sharding import Mesh, PartitionSpec as P

AX = ("x", "zh", "c", "zl", "y")
SIZES = dict(x=4, zh=2, c=2, zl=2, y=4)
BF = jnp.bfloat16
F32 = jnp.float32
HD = 128
HEADS = 8
SEQS = 8
ROWS = 32
LMAX = 2048
KB = 512
NB = LMAX // KB
D = 5120
DT = 640
BLK = 320
FT = 1664
NEG = -1e30
EPS = 1e-6
NC = 1
RR = 4 // NC
CR = 64 * RR
NH = 896
VM = pl.BlockSpec(memory_space=pltpu.VMEM)
SM = pl.BlockSpec(memory_space=pltpu.SMEM)
ANY = pl.BlockSpec(memory_space=pl.ANY)


def permute(value, axes, move):
    sizes = [SIZES[a] for a in axes]
    total = 1
    for n in sizes:
        total *= n
    pairs = []
    for i in range(total):
        coords, rest = [], i
        for n in reversed(sizes):
            coords.append(rest % n)
            rest //= n
        target = move(*reversed(coords))
        j = 0
        for n, q in zip(sizes, target):
            j = j * n + q
        pairs.append((i, j))
    return lax.ppermute(value, axes, pairs)


def along_x(value, k):
    return permute(value, ("x",), lambda x: ((x + k) % 4,))


def along_y(value, k):
    return permute(value, ("y",), lambda y: ((y + k) % 4,))


def along_z(value, k):
    def move(zh, zl):
        z = (zh * 2 + zl + k) % 4
        return (z // 2, z % 2)

    return permute(value, ("zh", "zl"), move)


def swap(value, axis):
    return permute(value, (axis,), lambda q: (1 - q,))


def one_hot(n, source):
    out = lax.broadcasted_iota(jnp.int32, (n, n), 0)
    src = lax.broadcasted_iota(jnp.int32, (n, n), 1)
    return (source(out) == src).astype(BF)


def spread(row):
    return row // RR % 8 * ROWS + row // (8 * RR) % 8 * 4 + row // CR * RR + row % RR


def gather(row):
    return row // RR % NC * CR + row // 4 % 8 * (8 * RR) + row // ROWS * RR + row % RR


def front_kernel(len_ref, q_ref, fresh_ref, res_ref, cache_ref, ow_ref, *refs):
    out_refs, (kv, ow, ctx, kv_sem, ow_sem) = refs[:NC], refs[NC:]
    def kv_copy(s, b):
        part = pl.ds(b * KB, KB)
        return pltpu.make_async_copy(
            cache_ref.at[s, :, part, :], kv.at[s, :, part, :], kv_sem.at[s, b]
        )

    for s in range(SEQS):
        for b in range(NB):

            @pl.when(b * KB < len_ref[s])
            def _(s=s, b=b):
                kv_copy(s, b).start()

    ow_copy = pltpu.make_async_copy(ow_ref, ow, ow_sem)
    ow_copy.start()
    factor = HD ** -0.5 * 1.4426950408889634
    nt = (((1,), (1,)), ((), ()))
    nn = (((1,), (0,)), ((), ()))

    def sequence(s, _):
        length = len_ref[s]
        rows = q_ref[s]
        q = jnp.concatenate([rows[:, h * HD : (h + 1) * HD] for h in range(HEADS)], axis=0)
        scores = lax.dot_general(q, fresh_ref[s, 0], nt, preferred_element_type=F32) * factor
        i = lax.broadcasted_iota(jnp.int32, scores.shape, 0) % ROWS
        j = lax.broadcasted_iota(jnp.int32, scores.shape, 1)
        scores = jnp.where(j <= i, scores, NEG)
        high = jnp.max(scores, axis=1, keepdims=True)
        p = jnp.exp2(scores - high)
        total = jnp.sum(p, axis=1, keepdims=True)
        acc = lax.dot_general(p.astype(BF), fresh_ref[s, 1], nn, preferred_element_type=F32)

        def block(b, carry):
            high, total, acc = carry
            kv_copy(s, b).wait()
            start = pl.multiple_of(b * KB, KB)
            k = kv[s, 0, pl.ds(start, KB), :]
            v = kv[s, 1, pl.ds(start, KB), :]
            scores = lax.dot_general(q, k, nt, preferred_element_type=F32) * factor
            pos = lax.broadcasted_iota(jnp.int32, scores.shape, 1)
            scores = jnp.where(pos < length - start, scores, NEG)
            new = jnp.maximum(high, jnp.max(scores, axis=1, keepdims=True))
            old = jnp.exp2(high - new)
            p = jnp.exp2(scores - new)
            total = total * old + jnp.sum(p, axis=1, keepdims=True)
            acc = acc * old + lax.dot_general(p.astype(BF), v, nn, preferred_element_type=F32)
            return new, total, acc

        high, total, acc = lax.fori_loop(0, (length + KB - 1) // KB, block, (high, total, acc))
        done = (acc / total).astype(BF)
        at = pl.ds(pl.multiple_of(s * ROWS, ROWS), ROWS)
        for h in range(HEADS):
            ctx[at, h * HD : (h + 1) * HD] = done[h * ROWS : (h + 1) * ROWS, :]
        return 0

    lax.fori_loop(0, SEQS, sequence, 0)
    hot = one_hot(256, spread)
    mixed = jnp.dot(hot, ctx[...], preferred_element_type=F32).astype(BF)
    residual = jnp.dot(hot, res_ref[...], preferred_element_type=F32)
    ow_copy.wait()
    for t in range(8):
        terms = jnp.dot(mixed, ow[:, t * DT : (t + 1) * DT], preferred_element_type=F32)
        terms = (terms + jnp.where(len_ref[SEQS] == t, residual, 0.0)).astype(BF)
        for q in range(NC):
            out_refs[q][t] = terms[q * CR : (q + 1) * CR]


def front(lengths, queries, fresh, residual, cache, out_weight):
    return pl.pallas_call(
        front_kernel,
        out_shape=[jax.ShapeDtypeStruct((8, CR, DT), BF)] * NC,
        in_specs=[SM, VM, VM, VM, ANY, ANY],
        out_specs=[VM] * NC,
        scratch_shapes=[
            pltpu.VMEM((SEQS, 2, LMAX, HD), BF),
            pltpu.VMEM((1024, D), BF),
            pltpu.VMEM((256, 1024), BF),
            pltpu.SemaphoreType.DMA((SEQS, NB)),
            pltpu.SemaphoreType.DMA,
        ],
        compiler_params=pltpu.CompilerParams(vmem_limit_bytes=48 * 2**20),
        name="attend_project",
    )(lengths, queries, fresh, residual, cache, out_weight)


def assemble_kernel(pos_ref, block_ref, near_ref, far_ref, w_ref, sem):
    zh = pos_ref[0]
    copies = []
    for dz, source in enumerate((near_ref, far_ref)):
        for i in range(8):
            g = i // 2 * 4 + (zh + dz) % 2 * 2 + i % 2
            row = pl.multiple_of(block_ref[g] * BLK, BLK)
            copies.append(
                pltpu.make_async_copy(
                    source.at[i], w_ref.at[:, pl.ds(row, BLK), :], sem.at[dz * 8 + i]
                )
            )
    for copy in copies:
        copy.start()
    for copy in copies:
        copy.wait()


def assemble(pos, block_of, near, far):
    return pl.pallas_call(
        assemble_kernel,
        out_shape=pltpu.VMEM((2, D, NH), BF),
        in_specs=[SM, SM, ANY, ANY],
        out_specs=VM,
        scratch_shapes=[pltpu.SemaphoreType.DMA((16,))],
        compiler_params=pltpu.CompilerParams(vmem_limit_bytes=2**20),
        name="assemble_weights",
    )(pos, block_of, near, far)


def feed_kernel(pos_ref, src_ref, gain_ref, w, *refs):
    arrived, (out_ref, act, normed, act_sem) = refs[:16], refs[16:]
    zh, tp, z, y = (pos_ref[i] for i in range(4))
    half = CR // 2
    steps = (0, 3, 1, 2)
    pieces = []
    for h in range(2):
        group = arrived[h * 8 : h * 8 + 8]
        offsets = (0, 0, 3, 3, 1, 1, 2, 2)
        blocks = [
            (ref, k, offsets[n], n % 2 * 2 + k) for n, ref in enumerate(group) for k in range(2)
        ]
        for n, (ref, at, outer, j) in enumerate(blocks):
            dz, dy = (outer, steps[j]) if h == 0 else (steps[j], outer)
            zz = (z + dz) % 4
            row = pl.multiple_of(zz // 2 * CR + h * half, half)
            col = pl.multiple_of((zz % 2 * 4 + (y + dy) % 4) * DT, 128)
            pieces.append(
                pltpu.make_async_copy(
                    ref.at[at], act.at[pl.ds(row, half), pl.ds(col, DT)], act_sem.at[h * 16 + n]
                )
            )
    for copy in pieces:
        copy.start()

    tiles = ((0, 256), (256, 256), (512, 256), (768, 128))
    for copy in pieces:
        copy.wait()
    gain = gain_ref[...].astype(F32)
    for r in range(0, 2 * CR, 64):
        rows = act[r : r + 64, :].astype(F32)
        inverse = lax.rsqrt(jnp.sum(rows * rows, axis=1, keepdims=True) / D + EPS)
        normed[r : r + 64, :] = (rows * inverse * gain).astype(BF)
    lhs = normed[...]
    for at, size in tiles:
        g = jnp.dot(lhs, w[0, :, at : at + size], preferred_element_type=F32)
        u = jnp.dot(lhs, w[1, :, at : at + size], preferred_element_type=F32)
        out_ref[:, at : at + size] = (g / (1 + jnp.exp(-g)) * u).astype(BF)
    own = pl.multiple_of(tp * DT, 128)
    flag = zh == 0
    mid = act[:, pl.ds(pl.multiple_of(own + 256, 128), 128)]
    low = act[:, pl.ds(own, 256)]
    high = act[:, pl.ds(pl.multiple_of(own + 384, 128), 256)]
    out_ref[:, 896:1152] = jnp.where(flag, low.astype(F32), high.astype(F32)).astype(BF)

    @pl.when(jnp.logical_not(flag))
    def _():
        out_ref[:, 0:128] = mid

    hot = (src_ref[...] == lax.broadcasted_iota(jnp.int32, (2 * CR, 2 * CR), 1)).astype(BF)
    out_ref[...] = jnp.dot(hot, out_ref[...], preferred_element_type=F32).astype(BF)


def feed(pos, src, gain, w, arrived):
    return pl.pallas_call(
        feed_kernel,
        out_shape=jax.ShapeDtypeStruct((2 * CR, 1152), BF),
        in_specs=[SM, VM, VM, VM] + [ANY] * 16,
        out_specs=VM,
        scratch_shapes=[
            pltpu.VMEM((2 * CR, D), BF),
            pltpu.VMEM((2 * CR, D), BF),
            pltpu.SemaphoreType.DMA((32,)),
        ],
        compiler_params=pltpu.CompilerParams(vmem_limit_bytes=28 * 2**20),
        name="feed_forward",
    )(pos, src, gain, pltpu.with_memory_space_constraint(w, pltpu.VMEM), *arrived)


def finish_kernel(*refs):
    in_refs, (even_ref, gated_ref) = refs[:NC], refs[NC:]
    hot = one_hot(256, gather)
    halves = []
    for zh in range(2):
        rows = jnp.concatenate(
            [r[x * 4 + zh * 2 + c] for r in in_refs for x in range(4) for c in range(2)], axis=0
        )
        halves.append(jnp.dot(hot, rows, preferred_element_type=F32).astype(BF))
    a, b = halves
    gated_ref[:, 0:896] = a[:, 0:896]
    gated_ref[:, 896:1664] = b[:, 128:896]
    even_ref[:, 0:256] = a[:, 896:1152]
    even_ref[:, 256:384] = b[:, 0:128]
    even_ref[:, 384:640] = b[:, 896:1152]


def finish(parts):
    return pl.pallas_call(
        finish_kernel,
        out_shape=(jax.ShapeDtypeStruct((256, DT), BF), jax.ShapeDtypeStruct((256, FT), BF)),
        in_specs=[VM] * NC,
        out_specs=(VM, VM),
        compiler_params=pltpu.CompilerParams(vmem_limit_bytes=32 * 2**20),
        name="finish",
    )(*parts)


def per_device(
    residual, queries, cache_kv, fresh_kv, lengths, destination_place, out_weight, norm_gain, gate_up, block_of
):
    x, zh, c, zl, y = (lax.axis_index(a) for a in AX)
    pos = jnp.stack([zh, zl * 4 + y, zh * 2 + zl, y]).astype(jnp.int32)
    group = x * 4 + zh * 2 + c

    both = lax.optimization_barrier(gate_up.transpose(1, 0, 2))
    left, right = both[:, :, :NH], both[:, :, FT - NH :]
    own = jnp.where(zh == 0, left, right)
    other = jnp.where(zh == 0, right, left)
    near = lax.all_gather(own, ("x", "c"), axis=0)
    lower, upper = swap(other[:, :224], "zh"), swap(other[:, 224:], "zh")

    own_lengths = lax.dynamic_slice_in_dim(lengths, group * SEQS, SEQS, 0)
    scalars = jnp.concatenate([own_lengths, pos[1:2]])
    terms = front(scalars, queries, fresh_kv, residual, cache_kv, out_weight)
    lower, *terms = lax.optimization_barrier((lower, *terms))

    slots = lax.iota(jnp.int32, 128)
    seq = jnp.sum(
        jnp.where(destination_place[None, :] == slots[:, None], slots[None, :], 0), axis=1
    )
    g = seq // 8
    base = (g // 2 % 2) * CR + (g // 4 * 2 + g % 2) * (8 * RR) + seq % 8 * RR
    src = (base[:, None] + lax.iota(jnp.int32, RR)[None, :]).reshape(2 * CR, 1)
    gain = norm_gain.reshape(1, D)

    parts = []
    for q in range(NC):
        got = lax.all_to_all(terms[q], ("zl", "y"), 0, 0, tiled=True)
        even = jnp.sum(got.astype(F32), axis=0).astype(BF)
        if q == 0:
            upper, even = lax.optimization_barrier((upper, even))
            other = jnp.concatenate([lower, upper], axis=1)
            far = lax.all_gather(other, ("x", "c"), axis=0)
            w = assemble(pos, block_of, near, far)
        even = lax.all_to_all(even, ("x", "c"), 0, 0, tiled=True)
        h1, h2 = even[: CR // 2], even[CR // 2 :]
        p1 = [h1, along_y(h1, 1), along_y(h1, -1), along_y(h1, 2)]
        p2 = [h2, along_z(h2, 1), along_z(h2, -1), along_z(h2, 2)]
        stacks = [jnp.stack(p[k : k + 2]) for p in (p1, p2) for k in (0, 2)]
        lo1, hi1, lo2, hi2 = lax.optimization_barrier(stacks)
        early = [along_z(lo1, 1), along_z(hi1, -1), along_y(lo2, 1), along_y(hi2, -1)]
        late = [along_z(hi1, 1), along_z(lo1, -1), along_y(hi2, 1), along_y(lo2, -1)]
        early = lax.optimization_barrier(early)
        on = [along_z(early[0], 1), along_z(early[1], -1), along_y(early[2], 1), along_y(early[3], -1)]
        arrived = [lo1, hi1, early[0], late[0], late[1], early[1], on[0], on[1]]
        arrived += [lo2, hi2, early[2], late[2], late[3], early[3], on[2], on[3]]
        mixed = feed(pos, src, gain, w, arrived)
        parts.append(lax.all_to_all(mixed.reshape(16, 8 * RR, 1152), ("x", "zh", "c"), 0, 0, tiled=True))
    return finish(parts)


def solution(mesh):
    inner = Mesh(mesh.devices.reshape(tuple(SIZES[a] for a in AX)), AX)
    grp, tp = ("x", "zh", "c"), ("zl", "y")
    return jax.shard_map(
        per_device,
        mesh=inner,
        in_specs=(
            P(grp, tp),
            P(grp, None, tp),
            P(grp, None, None, tp),
            P(grp, None, None, tp),
            P(),
            P(),
            P(tp, None),
            P(),
            P(grp, None, tp),
            P(),
        ),
        out_specs=(P(grp, tp), P(grp, tp)),
        check_vma=False,
    )
```

```python
import functools

import jax
import jax.numpy as jnp
from jax import lax
from jax.experimental import pallas as pl
from jax.experimental.pallas import tpu as pltpu
from jax.sharding import Mesh, PartitionSpec as P

AX = ("x", "zh", "c", "zl", "y")
SIZES = dict(x=4, zh=2, c=2, zl=2, y=4)
BF = jnp.bfloat16
F32 = jnp.float32
HD = 128
HEADS = 8
SEQS = 8
ROWS = 32
LMAX = 2048
KB = 512
NB = LMAX // KB
D = 5120
DT = 640
BLK = 320
FT = 1664
NEG = -1e30
EPS = 1e-6
NC = 1
RR = 4 // NC
CR = 64 * RR
NH = 896
VM = pl.BlockSpec(memory_space=pltpu.VMEM)
SM = pl.BlockSpec(memory_space=pltpu.SMEM)
ANY = pl.BlockSpec(memory_space=pl.ANY)


def permute(value, axes, move):
    sizes = [SIZES[a] for a in axes]
    total = 1
    for n in sizes:
        total *= n
    pairs = []
    for i in range(total):
        coords, rest = [], i
        for n in reversed(sizes):
            coords.append(rest % n)
            rest //= n
        target = move(*reversed(coords))
        j = 0
        for n, q in zip(sizes, target):
            j = j * n + q
        pairs.append((i, j))
    return lax.ppermute(value, axes, pairs)


def along_x(value, k):
    return permute(value, ("x",), lambda x: ((x + k) % 4,))


def along_y(value, k):
    return permute(value, ("y",), lambda y: ((y + k) % 4,))


def along_z(value, k):
    def move(zh, zl):
        z = (zh * 2 + zl + k) % 4
        return (z // 2, z % 2)

    return permute(value, ("zh", "zl"), move)


def swap(value, axis):
    return permute(value, (axis,), lambda q: (1 - q,))


def one_hot(n, source):
    out = lax.broadcasted_iota(jnp.int32, (n, n), 0)
    src = lax.broadcasted_iota(jnp.int32, (n, n), 1)
    return (source(out) == src).astype(BF)


def spread(row):
    return row // RR % 8 * ROWS + row // (8 * RR) % 8 * 4 + row // CR * RR + row % RR


def gather(row):
    return row // RR % NC * CR + row // 4 % 8 * (8 * RR) + row // ROWS * RR + row % RR


def front_kernel(len_ref, q_ref, fresh_ref, res_ref, cache_ref, ow_ref, *refs):
    out_refs, (kv, ow, ctx, kv_sem, ow_sem) = refs[:NC], refs[NC:]
    def kv_copy(s, b):
        part = pl.ds(b * KB, KB)
        return pltpu.make_async_copy(
            cache_ref.at[s, :, part, :], kv.at[s, :, part, :], kv_sem.at[s, b]
        )

    for s in range(SEQS):
        for b in range(NB):

            @pl.when(b * KB < len_ref[s])
            def _(s=s, b=b):
                kv_copy(s, b).start()

    ow_copy = pltpu.make_async_copy(ow_ref, ow, ow_sem)
    ow_copy.start()
    factor = HD ** -0.5 * 1.4426950408889634
    nt = (((1,), (1,)), ((), ()))
    nn = (((1,), (0,)), ((), ()))

    def sequence(s, _):
        length = len_ref[s]
        rows = q_ref[s]
        q = jnp.concatenate([rows[:, h * HD : (h + 1) * HD] for h in range(HEADS)], axis=0)
        scores = lax.dot_general(q, fresh_ref[s, 0], nt, preferred_element_type=F32) * factor
        i = lax.broadcasted_iota(jnp.int32, scores.shape, 0) % ROWS
        j = lax.broadcasted_iota(jnp.int32, scores.shape, 1)
        scores = jnp.where(j <= i, scores, NEG)
        high = jnp.max(scores, axis=1, keepdims=True)
        p = jnp.exp2(scores - high)
        total = jnp.sum(p, axis=1, keepdims=True)
        acc = lax.dot_general(p.astype(BF), fresh_ref[s, 1], nn, preferred_element_type=F32)

        def block(b, carry, last=False):
            high, total, acc = carry
            kv_copy(s, b).wait()
            start = pl.multiple_of(b * KB, KB)
            k = kv[s, 0, pl.ds(start, KB), :]
            v = kv[s, 1, pl.ds(start, KB), :]
            scores = lax.dot_general(q, k, nt, preferred_element_type=F32) * factor
            if last:
                pos = lax.broadcasted_iota(jnp.int32, scores.shape, 1)
                scores = jnp.where(pos < length - start, scores, NEG)
            new = jnp.maximum(high, jnp.max(scores, axis=1, keepdims=True))
            old = jnp.exp2(high - new)
            p = jnp.exp2(scores - new)
            total = total * old + jnp.sum(p, axis=1, keepdims=True)
            acc = acc * old + lax.dot_general(p.astype(BF), v, nn, preferred_element_type=F32)
            return new, total, acc

        full = (length - 1) // KB
        carry = lax.fori_loop(0, full, block, (high, total, acc))
        high, total, acc = block(full, carry, last=True)
        done = (acc / total).astype(BF)
        at = pl.ds(pl.multiple_of(s * ROWS, ROWS), ROWS)
        for h in range(HEADS):
            ctx[at, h * HD : (h + 1) * HD] = done[h * ROWS : (h + 1) * ROWS, :]
        return 0

    lax.fori_loop(0, SEQS, sequence, 0)
    hot = one_hot(256, spread)
    mixed = jnp.dot(hot, ctx[...], preferred_element_type=F32).astype(BF)
    residual = jnp.dot(hot, res_ref[...], preferred_element_type=F32)
    ow_copy.wait()
    for t in range(0, 8, 2):
        terms = jnp.dot(mixed, ow[:, t * DT : (t + 2) * DT], preferred_element_type=F32)
        for i in range(2):
            part = terms[:, i * DT : (i + 1) * DT]
            own = jnp.where(len_ref[SEQS] == t + i, residual, 0.0)
            out_refs[0][t + i] = (part + own).astype(BF)


def front(lengths, queries, fresh, residual, cache, out_weight):
    return pl.pallas_call(
        front_kernel,
        out_shape=[jax.ShapeDtypeStruct((8, CR, DT), BF)] * NC,
        in_specs=[SM, VM, VM, VM, ANY, ANY],
        out_specs=[VM] * NC,
        scratch_shapes=[
            pltpu.VMEM((SEQS, 2, LMAX, HD), BF),
            pltpu.VMEM((1024, D), BF),
            pltpu.VMEM((256, 1024), BF),
            pltpu.SemaphoreType.DMA((SEQS, NB)),
            pltpu.SemaphoreType.DMA,
        ],
        compiler_params=pltpu.CompilerParams(vmem_limit_bytes=48 * 2**20),
        name="attend_project",
    )(lengths, queries, fresh, residual, cache, out_weight)


def assemble_kernel(pos_ref, block_ref, near_ref, far_ref, w_ref, sem):
    zh = pos_ref[0]
    copies = []
    for dz, source in enumerate((near_ref, far_ref)):
        for i in range(8):
            g = i // 2 * 4 + (zh + dz) % 2 * 2 + i % 2
            row = pl.multiple_of(block_ref[g] * BLK, BLK)
            copies.append(
                pltpu.make_async_copy(
                    source.at[i], w_ref.at[:, pl.ds(row, BLK), :], sem.at[dz * 8 + i]
                )
            )
    for copy in copies:
        copy.start()
    for copy in copies:
        copy.wait()


def assemble(pos, block_of, near, far):
    return pl.pallas_call(
        assemble_kernel,
        out_shape=pltpu.VMEM((2, D, NH), BF),
        in_specs=[SM, SM, ANY, ANY],
        out_specs=VM,
        scratch_shapes=[pltpu.SemaphoreType.DMA((16,))],
        compiler_params=pltpu.CompilerParams(vmem_limit_bytes=2**20),
        name="assemble_weights",
    )(pos, block_of, near, far)


def feed_kernel(pos_ref, src_ref, gain_ref, w, *refs):
    arrived, (out_ref, act, normed, act_sem) = refs[:16], refs[16:]
    zh, tp, z, y = (pos_ref[i] for i in range(4))
    half = CR // 2
    steps = (0, 3, 1, 2)
    pieces = []
    for h in range(2):
        group = arrived[h * 8 : h * 8 + 8]
        offsets = (0, 0, 3, 3, 1, 1, 2, 2)
        blocks = [
            (ref, k, offsets[n], n % 2 * 2 + k) for n, ref in enumerate(group) for k in range(2)
        ]
        for n, (ref, at, outer, j) in enumerate(blocks):
            dz, dy = (outer, steps[j]) if h == 0 else (steps[j], outer)
            zz = (z + dz) % 4
            row = pl.multiple_of(zz // 2 * CR + h * half, half)
            col = pl.multiple_of((zz % 2 * 4 + (y + dy) % 4) * DT, 128)
            pieces.append(
                pltpu.make_async_copy(
                    ref.at[at], act.at[pl.ds(row, half), pl.ds(col, DT)], act_sem.at[h * 16 + n]
                )
            )
    for copy in pieces:
        copy.start()

    tiles = ((0, 256), (256, 256), (512, 256), (768, 128))
    for copy in pieces:
        copy.wait()
    gain = gain_ref[...].astype(F32)
    for r in range(0, 2 * CR, 64):
        rows = act[r : r + 64, :].astype(F32)
        inverse = lax.rsqrt(jnp.sum(rows * rows, axis=1, keepdims=True) / D + EPS)
        normed[r : r + 64, :] = (rows * inverse * gain).astype(BF)
    lhs = normed[...]
    for at, size in tiles:
        g = jnp.dot(lhs, w[0, :, at : at + size], preferred_element_type=F32)
        u = jnp.dot(lhs, w[1, :, at : at + size], preferred_element_type=F32)
        out_ref[:, at : at + size] = (g / (1 + jnp.exp(-g)) * u).astype(BF)
    own = pl.multiple_of(tp * DT, 128)
    flag = zh == 0
    mid = act[:, pl.ds(pl.multiple_of(own + 256, 128), 128)]
    low = act[:, pl.ds(own, 256)]
    high = act[:, pl.ds(pl.multiple_of(own + 384, 128), 256)]
    out_ref[:, 896:1152] = jnp.where(flag, low.astype(F32), high.astype(F32)).astype(BF)

    @pl.when(jnp.logical_not(flag))
    def _():
        out_ref[:, 0:128] = mid

    hot = (src_ref[...] == lax.broadcasted_iota(jnp.int32, (2 * CR, 2 * CR), 1)).astype(BF)
    out_ref[...] = jnp.dot(hot, out_ref[...], preferred_element_type=F32).astype(BF)


def feed(pos, src, gain, w, arrived):
    return pl.pallas_call(
        feed_kernel,
        out_shape=jax.ShapeDtypeStruct((2 * CR, 1152), BF),
        in_specs=[SM, VM, VM, VM] + [ANY] * 16,
        out_specs=VM,
        scratch_shapes=[
            pltpu.VMEM((2 * CR, D), BF),
            pltpu.VMEM((2 * CR, D), BF),
            pltpu.SemaphoreType.DMA((32,)),
        ],
        compiler_params=pltpu.CompilerParams(vmem_limit_bytes=28 * 2**20),
        name="feed_forward",
    )(pos, src, gain, pltpu.with_memory_space_constraint(w, pltpu.VMEM), *arrived)


def finish_kernel(*refs):
    in_refs, (even_ref, gated_ref) = refs[:NC], refs[NC:]
    hot = one_hot(256, gather)
    halves = []
    for zh in range(2):
        rows = jnp.concatenate(
            [r[x * 4 + zh * 2 + c] for r in in_refs for x in range(4) for c in range(2)], axis=0
        )
        halves.append(jnp.dot(hot, rows, preferred_element_type=F32).astype(BF))
    a, b = halves
    gated_ref[:, 0:896] = a[:, 0:896]
    gated_ref[:, 896:1664] = b[:, 128:896]
    even_ref[:, 0:256] = a[:, 896:1152]
    even_ref[:, 256:384] = b[:, 0:128]
    even_ref[:, 384:640] = b[:, 896:1152]


def finish(parts):
    return pl.pallas_call(
        finish_kernel,
        out_shape=(jax.ShapeDtypeStruct((256, DT), BF), jax.ShapeDtypeStruct((256, FT), BF)),
        in_specs=[VM] * NC,
        out_specs=(VM, VM),
        compiler_params=pltpu.CompilerParams(vmem_limit_bytes=32 * 2**20),
        name="finish",
    )(*parts)


def per_device(
    residual, queries, cache_kv, fresh_kv, lengths, destination_place, out_weight, norm_gain, gate_up, block_of
):
    x, zh, c, zl, y = (lax.axis_index(a) for a in AX)
    pos = jnp.stack([zh, zl * 4 + y, zh * 2 + zl, y]).astype(jnp.int32)
    group = x * 4 + zh * 2 + c

    both = lax.optimization_barrier(gate_up.transpose(1, 0, 2))
    left, right = both[:, :, :NH], both[:, :, FT - NH :]
    own = jnp.where(zh == 0, left, right)
    other = jnp.where(zh == 0, right, left)
    near = lax.all_gather(own, ("x", "c"), axis=0)
    lower, upper = swap(other[:, :224], "zh"), swap(other[:, 224:], "zh")

    own_lengths = lax.dynamic_slice_in_dim(lengths, group * SEQS, SEQS, 0)
    scalars = jnp.concatenate([own_lengths, pos[1:2]])
    terms = front(scalars, queries, fresh_kv, residual, cache_kv, out_weight)
    lower, *terms = lax.optimization_barrier((lower, *terms))

    slots = lax.iota(jnp.int32, 128)
    seq = jnp.sum(
        jnp.where(destination_place[None, :] == slots[:, None], slots[None, :], 0), axis=1
    )
    g = seq // 8
    base = (g // 2 % 2) * CR + (g // 4 * 2 + g % 2) * (8 * RR) + seq % 8 * RR
    src = (base[:, None] + lax.iota(jnp.int32, RR)[None, :]).reshape(2 * CR, 1)
    gain = norm_gain.reshape(1, D)

    parts = []
    for q in range(NC):
        got = lax.all_to_all(terms[q], ("zl", "y"), 0, 0, tiled=True)
        even = jnp.sum(got.astype(F32), axis=0).astype(BF)
        if q == 0:
            upper, even = lax.optimization_barrier((upper, even))
            other = jnp.concatenate([lower, upper], axis=1)
            far = lax.all_gather(other, ("x", "c"), axis=0)
            w = assemble(pos, block_of, near, far)
        even = lax.all_to_all(even, ("x", "c"), 0, 0, tiled=True)
        h1, h2 = even[: CR // 2], even[CR // 2 :]
        p1 = [h1, along_y(h1, 1), along_y(h1, -1), along_y(h1, 2)]
        p2 = [h2, along_z(h2, 1), along_z(h2, -1), along_z(h2, 2)]
        stacks = [jnp.stack(p[k : k + 2]) for p in (p1, p2) for k in (0, 2)]
        lo1, hi1, lo2, hi2 = lax.optimization_barrier(stacks)
        early = [along_z(lo1, 1), along_z(hi1, -1), along_y(lo2, 1), along_y(hi2, -1)]
        late = [along_z(hi1, 1), along_z(lo1, -1), along_y(hi2, 1), along_y(lo2, -1)]
        early = lax.optimization_barrier(early)
        on = [along_z(early[0], 1), along_z(early[1], -1), along_y(early[2], 1), along_y(early[3], -1)]
        arrived = [lo1, hi1, early[0], late[0], late[1], early[1], on[0], on[1]]
        arrived += [lo2, hi2, early[2], late[2], late[3], early[3], on[2], on[3]]
        mixed = feed(pos, src, gain, w, arrived)
        parts.append(lax.all_to_all(mixed.reshape(16, 8 * RR, 1152), ("x", "zh", "c"), 0, 0, tiled=True))
    return finish(parts)


def solution(mesh):
    inner = Mesh(mesh.devices.reshape(tuple(SIZES[a] for a in AX)), AX)
    grp, tp = ("x", "zh", "c"), ("zl", "y")
    return jax.shard_map(
        per_device,
        mesh=inner,
        in_specs=(
            P(grp, tp),
            P(grp, None, tp),
            P(grp, None, None, tp),
            P(grp, None, None, tp),
            P(),
            P(),
            P(tp, None),
            P(),
            P(grp, None, tp),
            P(),
        ),
        out_specs=(P(grp, tp), P(grp, tp)),
        check_vma=False,
    )
```

```python
import functools

import jax
import jax.numpy as jnp
from jax import lax
from jax.experimental import pallas as pl
from jax.experimental.pallas import tpu as pltpu
from jax.sharding import Mesh, PartitionSpec as P

AX = ("x", "zh", "c", "zl", "y")
SIZES = dict(x=4, zh=2, c=2, zl=2, y=4)
BF = jnp.bfloat16
F32 = jnp.float32
HD = 128
HEADS = 8
SEQS = 8
ROWS = 32
LMAX = 2048
KB = 512
NB = LMAX // KB
D = 5120
DT = 640
BLK = 320
FT = 1664
NEG = -1e30
EPS = 1e-6
NC = 1
RR = 4 // NC
CR = 64 * RR
NH = 896
VM = pl.BlockSpec(memory_space=pltpu.VMEM)
SM = pl.BlockSpec(memory_space=pltpu.SMEM)
ANY = pl.BlockSpec(memory_space=pl.ANY)


def permute(value, axes, move):
    sizes = [SIZES[a] for a in axes]
    total = 1
    for n in sizes:
        total *= n
    pairs = []
    for i in range(total):
        coords, rest = [], i
        for n in reversed(sizes):
            coords.append(rest % n)
            rest //= n
        target = move(*reversed(coords))
        j = 0
        for n, q in zip(sizes, target):
            j = j * n + q
        pairs.append((i, j))
    return lax.ppermute(value, axes, pairs)


def along_x(value, k):
    return permute(value, ("x",), lambda x: ((x + k) % 4,))


def along_y(value, k):
    return permute(value, ("y",), lambda y: ((y + k) % 4,))


def along_z(value, k):
    def move(zh, zl):
        z = (zh * 2 + zl + k) % 4
        return (z // 2, z % 2)

    return permute(value, ("zh", "zl"), move)


def swap(value, axis):
    return permute(value, (axis,), lambda q: (1 - q,))


def one_hot(n, source):
    out = lax.broadcasted_iota(jnp.int32, (n, n), 0)
    src = lax.broadcasted_iota(jnp.int32, (n, n), 1)
    return (source(out) == src).astype(BF)


def spread(row):
    return row // RR % 8 * ROWS + row // (8 * RR) % 8 * 4 + row // CR * RR + row % RR


def gather(row):
    return row // RR % NC * CR + row // 4 % 8 * (8 * RR) + row // ROWS * RR + row % RR


def front_kernel(len_ref, q_ref, fresh_ref, res_ref, cache_ref, ow_ref, *refs):
    out_refs, (kv, ow, ctx, kv_sem, ow_sem) = refs[:NC], refs[NC:]
    def kv_copy(s, b):
        part = pl.ds(b * KB, KB)
        return pltpu.make_async_copy(
            cache_ref.at[s, :, part, :], kv.at[s, :, part, :], kv_sem.at[s, b]
        )

    for s in range(SEQS):
        for b in range(NB):

            @pl.when(b * KB < len_ref[s])
            def _(s=s, b=b):
                kv_copy(s, b).start()

    ow_copy = pltpu.make_async_copy(ow_ref, ow, ow_sem)
    ow_copy.start()
    factor = HD ** -0.5 * 1.4426950408889634
    nt = (((1,), (1,)), ((), ()))
    nn = (((1,), (0,)), ((), ()))

    def sequence(s, _):
        length = len_ref[s]
        rows = q_ref[s]
        q = jnp.concatenate([rows[:, h * HD : (h + 1) * HD] for h in range(HEADS)], axis=0)
        scores = lax.dot_general(q, fresh_ref[s, 0], nt, preferred_element_type=F32) * factor
        i = lax.broadcasted_iota(jnp.int32, scores.shape, 0) % ROWS
        j = lax.broadcasted_iota(jnp.int32, scores.shape, 1)
        scores = jnp.where(j <= i, scores, NEG)
        high = jnp.max(scores, axis=1, keepdims=True)
        p = jnp.exp2(scores - high)
        total = jnp.sum(p, axis=1, keepdims=True)
        acc = lax.dot_general(p.astype(BF), fresh_ref[s, 1], nn, preferred_element_type=F32)

        def block(b, carry, last=False):
            high, total, acc = carry
            kv_copy(s, b).wait()
            start = pl.multiple_of(b * KB, KB)
            k = kv[s, 0, pl.ds(start, KB), :]
            v = kv[s, 1, pl.ds(start, KB), :]
            scores = lax.dot_general(q, k, nt, preferred_element_type=F32) * factor
            if last:
                pos = lax.broadcasted_iota(jnp.int32, scores.shape, 1)
                scores = jnp.where(pos < length - start, scores, NEG)
            new = jnp.maximum(high, jnp.max(scores, axis=1, keepdims=True))
            old = jnp.exp2(high - new)
            p = jnp.exp2(scores - new)
            total = total * old + jnp.sum(p, axis=1, keepdims=True)
            acc = acc * old + lax.dot_general(p.astype(BF), v, nn, preferred_element_type=F32)
            return new, total, acc

        full = (length - 1) // KB
        carry = lax.fori_loop(0, full, block, (high, total, acc))
        high, total, acc = block(full, carry, last=True)
        done = (acc / total).astype(BF)
        at = pl.ds(pl.multiple_of(s * ROWS, ROWS), ROWS)
        for h in range(HEADS):
            ctx[at, h * HD : (h + 1) * HD] = done[h * ROWS : (h + 1) * ROWS, :]
        return 0

    lax.fori_loop(0, SEQS, sequence, 0)
    hot = one_hot(256, spread)
    mixed = jnp.dot(hot, ctx[...], preferred_element_type=F32).astype(BF)
    residual = jnp.dot(hot, res_ref[...], preferred_element_type=F32)
    ow_copy.wait()
    for t in range(0, 8, 2):
        terms = jnp.dot(mixed, ow[:, t * DT : (t + 2) * DT], preferred_element_type=F32)
        for i in range(2):
            part = terms[:, i * DT : (i + 1) * DT]
            own = jnp.where(len_ref[SEQS] == t + i, residual, 0.0)
            out_refs[0][t + i] = (part + own).astype(BF)


def front(lengths, queries, fresh, residual, cache, out_weight):
    return pl.pallas_call(
        front_kernel,
        out_shape=[jax.ShapeDtypeStruct((8, CR, DT), BF)] * NC,
        in_specs=[SM, VM, VM, VM, ANY, ANY],
        out_specs=[VM] * NC,
        scratch_shapes=[
            pltpu.VMEM((SEQS, 2, LMAX, HD), BF),
            pltpu.VMEM((1024, D), BF),
            pltpu.VMEM((256, 1024), BF),
            pltpu.SemaphoreType.DMA((SEQS, NB)),
            pltpu.SemaphoreType.DMA,
        ],
        compiler_params=pltpu.CompilerParams(vmem_limit_bytes=48 * 2**20),
        name="attend_project",
    )(lengths, queries, fresh, residual, cache, out_weight)


def assemble_kernel(pos_ref, block_ref, near_ref, far_ref, w_ref, sem):
    zh = pos_ref[0]
    copies = []
    for dz, source in enumerate((near_ref, far_ref)):
        for i in range(8):
            g = i // 2 * 4 + (zh + dz) % 2 * 2 + i % 2
            row = pl.multiple_of(block_ref[g] * BLK, BLK)
            copies.append(
                pltpu.make_async_copy(
                    source.at[i], w_ref.at[:, pl.ds(row, BLK), :], sem.at[dz * 8 + i]
                )
            )
    for copy in copies:
        copy.start()
    for copy in copies:
        copy.wait()


def assemble(pos, block_of, near, far):
    return pl.pallas_call(
        assemble_kernel,
        out_shape=pltpu.VMEM((2, D, NH), BF),
        in_specs=[SM, SM, ANY, ANY],
        out_specs=VM,
        scratch_shapes=[pltpu.SemaphoreType.DMA((16,))],
        compiler_params=pltpu.CompilerParams(vmem_limit_bytes=2**20),
        name="assemble_weights",
    )(pos, block_of, near, far)


def feed_kernel(pos_ref, src_ref, gain_ref, w, *refs):
    arrived, (out_ref, act, normed, act_sem) = refs[:16], refs[16:]
    zh, tp, z, y = (pos_ref[i] for i in range(4))
    half = CR // 2
    steps = (0, 3, 1, 2)
    pieces = []
    for h in range(2):
        group = arrived[h * 8 : h * 8 + 8]
        offsets = (0, 0, 3, 3, 1, 1, 2, 2)
        blocks = [
            (ref, k, offsets[n], n % 2 * 2 + k) for n, ref in enumerate(group) for k in range(2)
        ]
        for n, (ref, at, outer, j) in enumerate(blocks):
            dz, dy = (outer, steps[j]) if h == 0 else (steps[j], outer)
            zz = (z + dz) % 4
            row = pl.multiple_of(zz // 2 * CR + h * half, half)
            col = pl.multiple_of((zz % 2 * 4 + (y + dy) % 4) * DT, 128)
            pieces.append(
                pltpu.make_async_copy(
                    ref.at[at], act.at[pl.ds(row, half), pl.ds(col, DT)], act_sem.at[h * 16 + n]
                )
            )
    for copy in pieces:
        copy.start()

    tiles = ((0, 256), (256, 256), (512, 256), (768, 128))
    for copy in pieces:
        copy.wait()
    gain = gain_ref[...].astype(F32)
    for r in range(0, 2 * CR, 64):
        rows = act[r : r + 64, :].astype(F32)
        inverse = lax.rsqrt(jnp.sum(rows * rows, axis=1, keepdims=True) / D + EPS)
        normed[r : r + 64, :] = (rows * inverse * gain).astype(BF)
    lhs = normed[...]
    for at, size in tiles:
        g = jnp.dot(lhs, w[0, :, at : at + size], preferred_element_type=F32)
        u = jnp.dot(lhs, w[1, :, at : at + size], preferred_element_type=F32)
        out_ref[:, at : at + size] = (g / (1 + jnp.exp(-g)) * u).astype(BF)
    own = pl.multiple_of(tp * DT, 128)
    flag = zh == 0
    mid = act[:, pl.ds(pl.multiple_of(own + 256, 128), 128)]
    low = act[:, pl.ds(own, 256)]
    high = act[:, pl.ds(pl.multiple_of(own + 384, 128), 256)]
    out_ref[:, 896:1152] = jnp.where(flag, low.astype(F32), high.astype(F32)).astype(BF)

    @pl.when(jnp.logical_not(flag))
    def _():
        out_ref[:, 0:128] = mid

    hot = (src_ref[...] == lax.broadcasted_iota(jnp.int32, (2 * CR, 2 * CR), 1)).astype(BF)
    out_ref[...] = jnp.dot(hot, out_ref[...], preferred_element_type=F32).astype(BF)


def feed(pos, src, gain, w, arrived):
    return pl.pallas_call(
        feed_kernel,
        out_shape=jax.ShapeDtypeStruct((2 * CR, 1152), BF),
        in_specs=[SM, VM, VM, VM] + [ANY] * 16,
        out_specs=VM,
        scratch_shapes=[
            pltpu.VMEM((2 * CR, D), BF),
            pltpu.VMEM((2 * CR, D), BF),
            pltpu.SemaphoreType.DMA((32,)),
        ],
        compiler_params=pltpu.CompilerParams(vmem_limit_bytes=28 * 2**20),
        name="feed_forward",
    )(pos, src, gain, pltpu.with_memory_space_constraint(w, pltpu.VMEM), *arrived)


def finish_kernel(*refs):
    in_refs, (even_ref, gated_ref) = refs[:NC], refs[NC:]
    hot = one_hot(256, gather)
    halves = []
    for zh in range(2):
        rows = jnp.concatenate(
            [r[x * 4 + zh * 2 + c] for r in in_refs for x in range(4) for c in range(2)], axis=0
        )
        halves.append(jnp.dot(hot, rows, preferred_element_type=F32).astype(BF))
    a, b = halves
    gated_ref[:, 0:896] = a[:, 0:896]
    gated_ref[:, 896:1664] = b[:, 128:896]
    even_ref[:, 0:256] = a[:, 896:1152]
    even_ref[:, 256:384] = b[:, 0:128]
    even_ref[:, 384:640] = b[:, 896:1152]


def finish(parts):
    return pl.pallas_call(
        finish_kernel,
        out_shape=(jax.ShapeDtypeStruct((256, DT), BF), jax.ShapeDtypeStruct((256, FT), BF)),
        in_specs=[VM] * NC,
        out_specs=(VM, VM),
        compiler_params=pltpu.CompilerParams(vmem_limit_bytes=32 * 2**20),
        name="finish",
    )(*parts)


def per_device(
    residual, queries, cache_kv, fresh_kv, lengths, destination_place, out_weight, norm_gain, gate_up, block_of
):
    x, zh, c, zl, y = (lax.axis_index(a) for a in AX)
    pos = jnp.stack([zh, zl * 4 + y, zh * 2 + zl, y]).astype(jnp.int32)
    group = x * 4 + zh * 2 + c

    both = lax.optimization_barrier(gate_up.transpose(1, 0, 2))
    left, right = both[:, :, :NH], both[:, :, FT - NH :]
    own = jnp.where(zh == 0, left, right)
    other = jnp.where(zh == 0, right, left)
    near = lax.all_gather(own, ("x", "c"), axis=0)
    lower, upper = swap(other[:, :192], "zh"), swap(other[:, 192:], "zh")

    own_lengths = lax.dynamic_slice_in_dim(lengths, group * SEQS, SEQS, 0)
    scalars = jnp.concatenate([own_lengths, pos[1:2]])
    terms = front(scalars, queries, fresh_kv, residual, cache_kv, out_weight)
    lower, *terms = lax.optimization_barrier((lower, *terms))

    slots = lax.iota(jnp.int32, 128)
    seq = jnp.sum(
        jnp.where(destination_place[None, :] == slots[:, None], slots[None, :], 0), axis=1
    )
    g = seq // 8
    base = (g // 2 % 2) * CR + (g // 4 * 2 + g % 2) * (8 * RR) + seq % 8 * RR
    src = (base[:, None] + lax.iota(jnp.int32, RR)[None, :]).reshape(2 * CR, 1)
    gain = norm_gain.reshape(1, D)

    parts = []
    for q in range(NC):
        got = lax.all_to_all(terms[q], ("zl", "y"), 0, 0, tiled=True)
        even = jnp.sum(got.astype(F32), axis=0).astype(BF)
        if q == 0:
            upper, even = lax.optimization_barrier((upper, even))
            other = jnp.concatenate([lower, upper], axis=1)
            far = lax.all_gather(other, ("x", "c"), axis=0)
            w = assemble(pos, block_of, near, far)
        even = lax.all_to_all(even, ("x", "c"), 0, 0, tiled=True)
        h1, h2 = even[: CR // 2], even[CR // 2 :]
        p1 = [h1, along_y(h1, 1), along_y(h1, -1), along_y(h1, 2)]
        p2 = [h2, along_z(h2, 1), along_z(h2, -1), along_z(h2, 2)]
        stacks = [jnp.stack(p[k : k + 2]) for p in (p1, p2) for k in (0, 2)]
        lo1, hi1, lo2, hi2 = lax.optimization_barrier(stacks)
        early = [along_z(lo1, 1), along_z(hi1, -1), along_y(lo2, 1), along_y(hi2, -1)]
        late = [along_z(hi1, 1), along_z(lo1, -1), along_y(hi2, 1), along_y(lo2, -1)]
        early = lax.optimization_barrier(early)
        on = [along_z(early[0], 1), along_z(early[1], -1), along_y(early[2], 1), along_y(early[3], -1)]
        arrived = [lo1, hi1, early[0], late[0], late[1], early[1], on[0], on[1]]
        arrived += [lo2, hi2, early[2], late[2], late[3], early[3], on[2], on[3]]
        mixed = feed(pos, src, gain, w, arrived)
        parts.append(lax.all_to_all(mixed.reshape(16, 8 * RR, 1152), ("x", "zh", "c"), 0, 0, tiled=True))
    return finish(parts)


def solution(mesh):
    inner = Mesh(mesh.devices.reshape(tuple(SIZES[a] for a in AX)), AX)
    grp, tp = ("x", "zh", "c"), ("zl", "y")
    return jax.shard_map(
        per_device,
        mesh=inner,
        in_specs=(
            P(grp, tp),
            P(grp, None, tp),
            P(grp, None, None, tp),
            P(grp, None, None, tp),
            P(),
            P(),
            P(tp, None),
            P(),
            P(grp, None, tp),
            P(),
        ),
        out_specs=(P(grp, tp), P(grp, tp)),
        check_vma=False,
    )
```
